32 devices in a mesh: dp: 8 (over y, x, core), tensor: 4 (over z).
Axes of the slice: x: 2, y: 2, z: 4, core: 2. Of those that a mesh axis runs over, the one named last changes fastest.
Arguments:
- hidden_in: bfloat16 [12288, 768], P(('dp', 'tensor')), may hold values from -6 to 6
- enc_states: bfloat16 [12288, 768], P(('dp', 'tensor')), may hold values from -6 to 6
- segments: int32 [12288], P('dp'), may hold values from 0 to 3, as said below
- dist_bucket: int32 [1536], replicated, may hold values from 0 to 31, as said below
- gain_self: float32 [768], replicated, may hold values from 0.1 to 1.9
- gain_cross: float32 [768], replicated, may hold values from 0.1 to 1.9
- gain_ff: float32 [768], replicated, may hold values from 0.1 to 1.9
- rel_table: float32 [32, 12], replicated, may hold values from -4 to 4
- self_query: bfloat16 [768, 768], P('dp', 'tensor'), may hold values from -0.02734375 to 0.02734375
- self_key: bfloat16 [768, 768], P('dp', 'tensor'), may hold values from -0.21875 to 0.21875
- self_value: bfloat16 [768, 768], P('dp', 'tensor'), may hold values from -0.21875 to 0.21875
- self_out: bfloat16 [768, 768], P('tensor', 'dp'), may hold values from -3.5 to 3.5
- cross_query: bfloat16 [768, 768], P('dp', 'tensor'), may hold values from -0.02734375 to 0.02734375
- cross_key: bfloat16 [768, 768], P('dp', 'tensor'), may hold values from -0.21875 to 0.21875
- cross_value: bfloat16 [768, 768], P('dp', 'tensor'), may hold values from -0.21875 to 0.21875
- cross_out: bfloat16 [768, 768], P('tensor', 'dp'), may hold values from -3.5 to 3.5
- ff_gate: bfloat16 [768, 2048], P('dp', 'tensor'), may hold values from -0.21875 to 0.21875
- ff_up: bfloat16 [768, 2048], P('dp', 'tensor'), may hold values from -0.21875 to 0.21875
- ff_down: bfloat16 [2048, 768], P('tensor', 'dp'), may hold values from -0.125 to 0.125
- d_out: bfloat16 [12288, 768], P(('dp', 'tensor')), may hold values from -7.2 to 7.2
Outputs:
- output: bfloat16 [12288, 768], P(('dp', 'tensor'))
- grad_hidden_in: bfloat16 [12288, 768], P(('dp', 'tensor'))
- grad_enc: bfloat16 [12288, 768], P(('dp', 'tensor'))
- grad_gain_self: float32 [768], replicated
- grad_gain_cross: float32 [768], replicated
- grad_gain_ff: float32 [768], replicated
- grad_rel_table: float32 [32, 12], replicated
- grad_self_query: float32 [768, 768], P('dp', 'tensor')
- grad_self_key: float32 [768, 768], P('dp', 'tensor')
- grad_self_value: float32 [768, 768], P('dp', 'tensor')
- grad_self_out: float32 [768, 768], P('tensor', 'dp')
- grad_cross_query: float32 [768, 768], P('dp', 'tensor')
- grad_cross_key: float32 [768, 768], P('dp', 'tensor')
- grad_cross_value: float32 [768, 768], P('dp', 'tensor')
- grad_cross_out: float32 [768, 768], P('tensor', 'dp')
- grad_ff_gate: float32 [768, 2048], P('dp', 'tensor')
- grad_ff_up: float32 [768, 2048], P('dp', 'tensor')
- grad_ff_down: float32 [2048, 768], P('tensor', 'dp')
The draws below stay inside these ranges and needn't reach their ends.
Inputs may be any that keep to these rules, and one draw needn't show every extreme that they name: `segments`: in each sequence of 1536 rows the numbers start at 0, never fall and end at 3; the document numbered 2 begins before row 384 of its sequence and ends at row 1152 or later. `dist_bucket`: distance 0 has bucket 0, buckets never fall as the distance grows, every bucket holds some distance below min(128, 1536), and from there on the bucket stays 32 - 1.
All inputs are finite; a program needn't handle non-finite values.
Results may differ from the reference program's by a relative error of at most 0.035.
Values may be sent and summed in bfloat16 or wider, within the bound.
A program may use at most 256 MiB of HBM per device.

```python
import jax
import jax.numpy as jnp
from jax import lax

D = 768
H = 12
DH = 64
FF = 2048
NB = 32
MAX_DIST = 128
TOK_DEV = 384
SEQ = 1536
TOKENS = 12288


def draw_segments(key, part):
    key = jax.random.fold_in(key, 11)
    first_key, second_key, third_key = jax.random.split(key, 3)
    sequences = TOKENS // SEQ
    opening = jax.random.randint(first_key, (sequences,), 2, TOK_DEV)
    splitter = jax.random.randint(second_key, (sequences,), 1, opening)
    closing = jax.random.randint(third_key, (sequences,), SEQ - TOK_DEV + 1, SEQ)
    places = jnp.arange(SEQ, dtype=jnp.int32)[None, :]
    numbers = (places >= splitter[:, None]).astype(jnp.int32) + (places >= opening[:, None]).astype(jnp.int32) + (places >= closing[:, None]).astype(jnp.int32)
    return numbers.reshape(TOKENS)


def draw_dist_bucket(key, part):
    key = jax.random.fold_in(key, 12)
    reach_span = min(MAX_DIST, SEQ)
    shuffled = jax.random.permutation(key, reach_span - 1).astype(jnp.int32) + 1
    breakpoints = shuffled[:NB - 1]
    distances = jnp.arange(SEQ, dtype=jnp.int32)
    return jnp.sum((distances[:, None] >= breakpoints[None, :]).astype(jnp.int32), axis=1).astype(jnp.int32)


def draw_d_out(key, part):
    key = jax.random.fold_in(key, 13)
    positions = jnp.arange(TOKENS, dtype=jnp.float32)
    rising = 0.6 + 1.2 * positions / max(TOKENS - 1, 1)
    values = jnp.clip(jax.random.normal(key, (TOKENS, D), jnp.float32), -4.0, 4.0)
    return (values * rising[:, None]).astype(jnp.bfloat16)


def levels(own_key, extent, shards, least, high):
    level = 1.0
    for axis_at, parts in shards:
        draws = jax.random.uniform(jax.random.fold_in(jax.random.fold_in(own_key, 6), axis_at), (parts,), jnp.float32, least / len(shards), high / len(shards))
        level = level * jnp.repeat(jnp.exp(draws), extent[axis_at] // parts).reshape((-1,) + (1,) * (len(extent) - 1 - axis_at))
    return level


def noise(own_key, dims, width, limit, cuts=(), kind=jnp.bfloat16):
    gain = levels(own_key, dims, cuts, -0.22, 0.18) if cuts else 1.0
    entries = jax.random.normal(own_key, dims, jnp.float32) * width * gain
    return jnp.minimum(jnp.maximum(entries, -limit), limit).astype(kind)


def setup_inputs(seed: int = 0) -> dict:
    splits = jax.random.split(jax.random.key(seed), 21)
    return {
        "hidden_in": noise(splits[0], (TOKENS, D), 1.0, 6.0, ((0, 32),)),
        "enc_states": noise(splits[1], (TOKENS, D), 1.0, 6.0, ((0, 32),)),
        "segments": draw_segments(jax.random.fold_in(splits[20], 71), 0),
        "dist_bucket": draw_dist_bucket(jax.random.fold_in(splits[20], 71), 0),
        "gain_self": jnp.clip(1.0 + 0.18 * jax.random.normal(splits[4], (D,), jnp.float32), 0.1, 1.9),
        "gain_cross": jnp.clip(1.0 + 0.18 * jax.random.normal(splits[5], (D,), jnp.float32), 0.1, 1.9),
        "gain_ff": jnp.clip(1.0 + 0.18 * jax.random.normal(splits[6], (D,), jnp.float32), 0.1, 1.9),
        "rel_table": noise(splits[7], (NB, H), 1.0, 4.0, (), jnp.float32),
        "self_query": noise(splits[8], (D, H * DH), (D * DH) ** -0.5, 0.02734375, ((0, 8), (1, 4))),
        "self_key": noise(splits[9], (D, H * DH), D ** -0.5, 0.21875, ((0, 8), (1, 4))),
        "self_value": noise(splits[10], (D, H * DH), D ** -0.5, 0.21875, ((0, 8), (1, 4))),
        "self_out": noise(splits[11], (H * DH, D), (max(1, H * DH // 256)) ** -0.5, 3.5, ((0, 4), (1, 8))),
        "cross_query": noise(splits[12], (D, H * DH), (D * DH) ** -0.5, 0.02734375, ((0, 8), (1, 4))),
        "cross_key": noise(splits[13], (D, H * DH), D ** -0.5, 0.21875, ((0, 8), (1, 4))),
        "cross_value": noise(splits[14], (D, H * DH), D ** -0.5, 0.21875, ((0, 8), (1, 4))),
        "cross_out": noise(splits[15], (H * DH, D), (max(1, H * DH // 256)) ** -0.5, 3.5, ((0, 4), (1, 8))),
        "ff_gate": noise(splits[16], (D, FF), D ** -0.5, 0.21875, ((0, 8), (1, 4))),
        "ff_up": noise(splits[17], (D, FF), D ** -0.5, 0.21875, ((0, 8), (1, 4))),
        "ff_down": noise(splits[18], (FF, D), FF ** -0.5, 0.125, ((0, 4), (1, 8))),
        "d_out": draw_d_out(jax.random.fold_in(splits[20], 71), 0),
    }


epsilon = 1e-06
masked_fill = -1e+30
highest = lax.Precision.HIGHEST

@jax.custom_vjp
def low(v):
    return lax.optimization_barrier(v.astype(jnp.bfloat16)).astype(jnp.float32)

@jax.custom_vjp
def low_back(v):
    return v

def low_keep(v):
    return (low(v), None)

def low_pass(kept, grad):
    return (grad,)

def back_keep(v):
    return (v, None)

def back_low(kept, grad):
    return (low(grad),)
low.defvjp(low_keep, low_pass)
low_back.defvjp(back_keep, back_low)

def matmul(left, right):
    return jnp.dot(left, right, precision=highest)

def rms_norm(row_data, norm_gain):
    return row_data * lax.rsqrt(lax.optimization_barrier(jnp.mean(row_data * row_data, axis=-1, keepdims=True)) + epsilon) * norm_gain

def attention(query, keys, values, segments, table, dist_bucket, causal):
    length = query.shape[0]
    rows_block = min(512, length)
    key_heads = keys.reshape(length, H, DH)
    value_heads = values.reshape(length, H, DH)
    query_blocks = query.reshape(length // rows_block, rows_block, H, DH)
    starts = jnp.arange(length // rows_block, dtype=jnp.int32) * rows_block

    def one_block(inputs):
        query_block, first_row = inputs
        row_index = first_row + jnp.arange(rows_block, dtype=jnp.int32)
        row_segments = lax.dynamic_slice_in_dim(segments, first_row, rows_block, 0)
        allowed = row_segments[:, None] == segments[None, :]
        scores = jnp.einsum('rhd,khd->hrk', query_block, key_heads, precision=highest)
        if causal:
            distance = row_index[:, None] - jnp.arange(length, dtype=jnp.int32)[None, :]
            allowed = allowed & (distance >= 0)
            picked = dist_bucket[jnp.clip(distance, 0, length - 1)]
            scores = scores + jnp.transpose(table[picked], (2, 0, 1))
        scores = low_back(scores)
        logits = jnp.where(allowed[None], scores, masked_fill)
        row_max = lax.optimization_barrier(jnp.max(logits, axis=-1, keepdims=True))
        weights = jnp.exp(logits - row_max)
        probability = weights / lax.optimization_barrier(jnp.sum(weights, axis=-1, keepdims=True))
        mixed_rows = jnp.einsum('hrk,khd->rhd', low(probability), value_heads, precision=highest)
        return mixed_rows.reshape(rows_block, H * DH)
    mixed_rows = lax.map(jax.checkpoint(one_block), (query_blocks, starts))
    return mixed_rows.reshape(length, H * DH)

def reference(hidden_in, enc_states, segments, dist_bucket, gain_self, gain_cross, gain_ff, rel_table, self_query, self_key, self_value, self_out, cross_query, cross_key, cross_value, cross_out, ff_gate, ff_up, ff_down, d_out):
    sequences = TOKENS // SEQ
    segment_rows = segments.reshape(sequences, SEQ)

    def forward(hidden, encoded, gain_one, gain_two, gain_three, table, query_one_w, key_one_w, value_one_w, out_one_w, query_two_w, key_two_w, value_two_w, out_two_w, gate_w, upper_w, down_w):

        def sequence(inputs):
            row_data, enc_rows, seg_rows = inputs
            norm_one = low(rms_norm(row_data, gain_one))
            query_one = low_back(low(matmul(norm_one, query_one_w)))
            key_one = low_back(low(matmul(norm_one, key_one_w)))
            value_one = low_back(low(matmul(norm_one, value_one_w)))
            attended_one = low_back(low(attention(query_one, key_one, value_one, seg_rows, table, dist_bucket, True)))
            mixed_one = row_data + low_back(matmul(attended_one, out_one_w))
            norm_two = low(rms_norm(mixed_one, gain_two))
            query_two = low_back(low(matmul(norm_two, query_two_w)))
            key_two = low_back(low(matmul(enc_rows, key_two_w)))
            value_two = low_back(low(matmul(enc_rows, value_two_w)))
            attended_two = low_back(low(attention(query_two, key_two, value_two, seg_rows, table, dist_bucket, False)))
            mixed_two = mixed_one + low_back(matmul(attended_two, out_two_w))
            norm_three = low(rms_norm(mixed_two, gain_three))
            gate_value = low_back(matmul(norm_three, gate_w))
            upper_value = low_back(matmul(norm_three, upper_w))
            hidden_value = low(jax.nn.gelu(gate_value, approximate=True) * upper_value)
            return mixed_two + low_back(matmul(hidden_value, down_w))
        result = lax.map(sequence, (hidden.reshape(sequences, SEQ, D), encoded.reshape(sequences, SEQ, D), segment_rows))
        return result.reshape(TOKENS, D)
    arguments = tuple((value.astype(jnp.float32) for value in (hidden_in, enc_states, gain_self, gain_cross, gain_ff, rel_table, self_query, self_key, self_value, self_out, cross_query, cross_key, cross_value, cross_out, ff_gate, ff_up, ff_down)))
    output, pullback = jax.vjp(forward, *arguments)
    gradients = pullback(d_out.astype(jnp.float32))
    return (output.astype(jnp.bfloat16), gradients[0].astype(jnp.bfloat16), gradients[1].astype(jnp.bfloat16), gradients[2], gradients[3], gradients[4], gradients[5], gradients[6], gradients[7], gradients[8], gradients[9], gradients[10], gradients[11], gradients[12], gradients[13], gradients[14], gradients[15], gradients[16])
```

```python
import functools

import jax
import jax.numpy as jnp
from jax import lax
from jax.experimental import pallas as pl
from jax.experimental.pallas import tpu as pltpu
from jax.sharding import PartitionSpec as P

DH = 64
QB = 256
REACH = 128
NEAR = QB + REACH

epsilon = 1e-06
masked_fill = -1e30


def matmul(left, right):
    return jnp.dot(left, right, preferred_element_type=jnp.float32)


def dot_nt(left, right):
    return lax.dot_general(
        left, right, (((1,), (1,)), ((), ())), preferred_element_type=jnp.float32
    )


def dot_tn(left, right):
    return lax.dot_general(
        left, right, (((0,), (0,)), ((), ())), preferred_element_type=jnp.float32
    )


def dot_tt(left, right):
    return lax.dot_general(
        left, right, (((0,), (1,)), ((), ())), preferred_element_type=jnp.float32
    )


def dot_rows(left, right_t):
    return lax.dot_general(
        left, right_t, (((0,), (1,)), ((), ())), preferred_element_type=jnp.float32
    )


def gelu_tanh(values):
    return jax.nn.gelu(values, approximate=True)


def rms_forward(row_data, norm_gain):
    inverse = lax.rsqrt(jnp.mean(row_data * row_data, axis=-1, keepdims=True) + epsilon)
    return ((row_data * inverse * norm_gain).astype(jnp.bfloat16), inverse)


def rms_backward(row_data, inverse, norm_gain, incoming):
    weighted = incoming * norm_gain
    inner = jnp.mean(weighted * row_data, axis=-1, keepdims=True)
    return inverse * weighted - row_data * (inverse * inverse * inverse) * inner


def head_lanes(head, width, lanes):
    lane = lax.broadcasted_iota(jnp.int32, (1, lanes), 1)
    own = (lane >= head * DH) & (lane < head * DH + DH)
    return (own | (lane >= width)).astype(jnp.float32).astype(jnp.bfloat16)


def band_distance(rows, columns):
    row = lax.broadcasted_iota(jnp.int32, (rows, columns), 0)
    column = lax.broadcasted_iota(jnp.int32, (rows, columns), 1)
    return column - row + REACH


def forward_kernel(causal, heads, *refs):
    if causal:
        first_ref, table_ref, q_ref, k_ref, vt_ref, ot_ref, sums_ref, band_ref = refs
        buckets = first_ref.shape[0]
        distance = band_distance(NEAR, QB)
        for head in range(heads):
            bias = jnp.full((NEAR, QB), table_ref[0, head], jnp.float32)
            for bucket in range(1, buckets):
                bias = jnp.where(distance >= first_ref[bucket], table_ref[bucket, head], bias)
            bias = bias - table_ref[buckets - 1, head]
            band_ref[head] = jnp.where(distance >= 0, bias, masked_fill)
    else:
        q_ref, k_ref, vt_ref, ot_ref, sums_ref = refs
        band_ref = None
    length, lanes = q_ref.shape
    width = heads * DH

    def block(first, far, near, head):
        query = q_ref[pl.ds(first, QB), :] * head_lanes(head, width, lanes)
        own = pl.ds(pl.multiple_of(head * DH, DH), DH)
        parts = []
        if far:
            parts.append((dot_nt(k_ref[0:far, :], query), 0, far))
        if near:
            scores = dot_nt(k_ref[far : far + near, :], query)
            parts.append((scores + band_ref[head, NEAR - near :, :], far, far + near))
        top = functools.reduce(
            jnp.maximum, [jnp.max(part[0], axis=0, keepdims=True) for part in parts]
        )
        total, mixed = 0.0, 0.0
        for scores, low, high in parts:
            weights = jnp.exp(scores - top)
            total = total + jnp.sum(weights, axis=0, keepdims=True)
            mixed = mixed + matmul(vt_ref[own, low:high], weights.astype(jnp.bfloat16))
        ot_ref[own, pl.ds(first, QB)] = (mixed / total).astype(jnp.bfloat16)
        sums_ref[head, :, pl.ds(first, QB)] = top + jnp.log(total)

    if causal:
        for at in range(length // QB):
            far = max(at * QB - REACH, 0)
            near = (at + 1) * QB - far

            def one(head, carry):
                block(at * QB, far, near, head)
                return carry

            lax.fori_loop(0, heads, one, 0)
    else:

        def one(step, carry):
            block(pl.multiple_of((step // heads) * QB, QB), length, 0, step % heads)
            return carry

        lax.fori_loop(0, heads * (length // QB), one, 0)


def backward_kernel(causal, heads, *refs):
    if causal:
        (first_ref, q_ref, k_ref, kt_ref, v_ref, e_ref, sums_ref, band_ref) = refs[:8]
        (dqt_ref, dk_ref, dv_ref, bucket_ref, key_total, value_total, near_total, far_total) = refs[8:]
        near_total[...] = jnp.zeros_like(near_total)
        far_total[...] = jnp.zeros_like(far_total)
    else:
        q_ref, k_ref, kt_ref, v_ref, e_ref, sums_ref = refs[:6]
        dqt_ref, dk_ref, dv_ref, key_total, value_total = refs[6:]
        band_ref = None
    length, lanes = q_ref.shape
    width = heads * DH
    key_total[...] = jnp.zeros_like(key_total)
    value_total[...] = jnp.zeros_like(value_total)

    def block(first, far, near, head):
        lane_mask = head_lanes(head, width, lanes)
        query = q_ref[pl.ds(first, QB), :] * lane_mask
        grad = e_ref[pl.ds(first, QB), :] * lane_mask
        own = pl.ds(pl.multiple_of(head * DH, DH), DH)
        sums = sums_ref[head, :, pl.ds(first, QB)]
        spans = []
        if far:
            spans.append((0, far, None))
        if near:
            spans.append((far, far + near, NEAR - near))
        delta, parts = 0.0, []
        for low, high, start in spans:
            scores = dot_nt(k_ref[low:high, :], query)
            if start is not None:
                scores = scores + band_ref[head, start:, :]
            chance = jnp.exp(scores - sums)
            pulled = dot_nt(v_ref[low:high, :], grad)
            delta = delta + jnp.sum(chance * pulled, axis=0, keepdims=True)
            value_total[low:high, :] += matmul(chance.astype(jnp.bfloat16), grad)
            parts.append((low, high, start, chance, pulled))
        moved = 0.0
        for low, high, start, chance, pulled in parts:
            slope = chance * (pulled - delta)
            if causal:
                if start is None:
                    far_total[head] += jnp.sum(slope, axis=0, keepdims=True)
                else:
                    near_total[head, start:, :] += slope
            slope = slope.astype(jnp.bfloat16)
            key_total[low:high, :] += matmul(slope, query)
            moved = moved + matmul(kt_ref[own, low:high], slope)
        dqt_ref[own, pl.ds(first, QB)] = moved.astype(jnp.bfloat16)

    if causal:
        for at in range(length // QB):
            far = max(at * QB - REACH, 0)
            near = (at + 1) * QB - far

            def one(head, carry):
                block(at * QB, far, near, head)
                return carry

            lax.fori_loop(0, heads, one, 0)
        distance = band_distance(2 * REACH, REACH)
        for head in range(heads):
            folded = near_total[head, 0 : 2 * REACH, 0:REACH] + near_total[head, REACH:NEAR, REACH:QB]
            away = far_total[head, :, 0:REACH] + far_total[head, :, REACH:QB]
            away = away + jnp.sum(near_total[head, 0:REACH, REACH:QB], axis=0, keepdims=True)
            for bucket in range(first_ref.shape[0]):
                reached = jnp.where(distance >= first_ref[bucket], folded, 0.0)
                bucket_ref[head, bucket : bucket + 1, :] = (
                    jnp.sum(reached, axis=0, keepdims=True) + away
                )
    else:

        def one(step, carry):
            block(pl.multiple_of((step // heads) * QB, QB), length, 0, step % heads)
            return carry

        lax.fori_loop(0, heads * (length // QB), one, 0)
    dk_ref[...] = key_total[...].astype(jnp.bfloat16)
    dv_ref[...] = value_total[...].astype(jnp.bfloat16)


VMEM = pl.BlockSpec(memory_space=pltpu.VMEM)
SMEM = pl.BlockSpec(memory_space=pltpu.SMEM)


def attend_forward(query, keys, value_t, heads, first=None, table=None):
    length = query.shape[0]
    causal = first is not None
    outs = [
        jax.ShapeDtypeStruct((heads * DH, length), jnp.bfloat16),
        jax.ShapeDtypeStruct((heads, 1, length), jnp.float32),
    ]
    args = [query, keys, value_t]
    specs = [VMEM] * 3
    if causal:
        outs.append(jax.ShapeDtypeStruct((heads, NEAR, QB), jnp.float32))
        args = [first, table] + args
        specs = [SMEM, SMEM] + specs
    pairs = length * length * heads // (2 if causal else 1)
    return pl.pallas_call(
        functools.partial(forward_kernel, causal, heads),
        out_shape=outs,
        in_specs=specs,
        out_specs=[VMEM] * len(outs),
        compiler_params=pltpu.CompilerParams(vmem_limit_bytes=48 * 2**20),
        cost_estimate=pl.CostEstimate(
            flops=pairs * 4 * DH * 8, bytes_accessed=4 * length * 512, transcendentals=pairs
        ),
        name="attend_self" if causal else "attend_cross",
    )(*args)


def attend_backward(query, keys, keys_t, values, grad, sums, heads, first=None, band=None):
    length, lanes = query.shape
    causal = first is not None
    outs = [
        jax.ShapeDtypeStruct((heads * DH, length), jnp.bfloat16),
        jax.ShapeDtypeStruct((length, lanes), jnp.bfloat16),
        jax.ShapeDtypeStruct((length, lanes), jnp.bfloat16),
    ]
    args = [query, keys, keys_t, values, grad, sums]
    specs = [VMEM] * 6
    scratch = [pltpu.VMEM((length, lanes), jnp.float32)] * 2
    if causal:
        outs.append(jax.ShapeDtypeStruct((heads, first.shape[0], REACH), jnp.float32))
        args = [first] + args + [band]
        specs = [SMEM] + specs + [VMEM]
        scratch = scratch + [
            pltpu.VMEM((heads, NEAR, QB), jnp.float32),
            pltpu.VMEM((heads, 1, QB), jnp.float32),
        ]
    pairs = length * length * heads // (2 if causal else 1)
    return pl.pallas_call(
        functools.partial(backward_kernel, causal, heads),
        out_shape=outs,
        in_specs=specs,
        out_specs=[VMEM] * len(outs),
        scratch_shapes=scratch,
        compiler_params=pltpu.CompilerParams(vmem_limit_bytes=56 * 2**20),
        cost_estimate=pl.CostEstimate(
            flops=pairs * 10 * DH * 8, bytes_accessed=9 * length * 512, transcendentals=pairs
        ),
        name="pull_self" if causal else "pull_cross",
    )(*args)


def gather_rows(row_data):
    return lax.all_gather(row_data, "tensor", axis=0, tiled=True)


def scatter_rows(terms):
    return lax.psum_scatter(
        terms.astype(jnp.bfloat16), "tensor", scatter_dimension=0, tiled=True
    ).astype(jnp.float32)


def scatter_grads(parts):
    joined = jnp.concatenate([part.astype(jnp.bfloat16) for part in parts], axis=1)
    return lax.psum_scatter(joined, "dp", scatter_dimension=0, tiled=True).astype(jnp.float32)


def local(
    hidden_in,
    enc_states,
    segments,
    dist_bucket,
    gain_self,
    gain_cross,
    gain_ff,
    rel_table,
    self_query,
    self_key,
    self_value,
    self_out,
    cross_query,
    cross_key,
    cross_value,
    cross_out,
    ff_gate,
    ff_up,
    ff_down,
    d_out,
):
    width = self_query.shape[1]
    heads = width // DH
    units = ff_gate.shape[1]
    rows = hidden_in.shape[0]
    place = lax.axis_index("tensor")
    first_row = place * rows
    table_heads = lax.dynamic_slice_in_dim(rel_table, place * heads, heads, 1)

    def own_rows(array):
        return lax.dynamic_slice_in_dim(array, first_row, rows, 0)

    first_weights = lax.all_gather(
        jnp.concatenate([self_query, self_key, self_value], axis=1), "dp", axis=0, tiled=True
    )
    base_all = gather_rows(hidden_in).astype(jnp.float32)
    enc_all = gather_rows(enc_states)
    swap_weights = lax.all_gather(
        jnp.concatenate([self_out.T, cross_out.T, cross_query], axis=1), "dp", axis=0, tiled=True
    )
    swap_full = lax.all_gather(swap_weights, "tensor", axis=0, tiled=False)
    rest_weights = lax.all_gather(
        jnp.concatenate([cross_key, cross_value, ff_gate, ff_up, ff_down.T], axis=1),
        "dp",
        axis=0,
        tiled=True,
    )
    cotangent_all = gather_rows(d_out)
    model = first_weights.shape[0]

    def full(at):
        picked = swap_full[:, :, at * width : (at + 1) * width]
        return jnp.transpose(picked, (1, 0, 2)).reshape(model, -1)

    self_out_t = swap_weights[:, :width]
    cross_out_t = swap_weights[:, width : 2 * width]
    cross_query_local = swap_weights[:, 2 * width :]
    self_out_full_t, cross_out_full_t, cross_query_full = full(0), full(1), full(2)
    cross_key_value = rest_weights[:, : 2 * width]
    gate_upper = rest_weights[:, 2 * width : 2 * width + 2 * units]
    down_t = rest_weights[:, 2 * width + 2 * units :]

    numbers = jnp.arange(-width % 128, dtype=jnp.int32)
    same = segments[:, None] == numbers[None, :]
    query_mark = same.astype(jnp.bfloat16)
    key_mark = jnp.where(same, 0.0, masked_fill).astype(jnp.bfloat16)
    blank = jnp.zeros_like(query_mark)
    buckets = rel_table.shape[0]
    first_distance = jnp.sum(
        (dist_bucket[None, :] < jnp.arange(buckets, dtype=jnp.int32)[:, None]).astype(jnp.int32),
        axis=1,
    )

    norm_one, inverse_one = rms_forward(base_all, gain_self)
    qkv = matmul(norm_one, first_weights).astype(jnp.bfloat16)
    query_one = jnp.concatenate([qkv[:, :width], query_mark], axis=1)
    key_one = jnp.concatenate([qkv[:, width : 2 * width], key_mark], axis=1)
    value_one = jnp.concatenate([qkv[:, 2 * width :], blank], axis=1)
    kept_one, sums_one, band = attend_forward(
        query_one, key_one, qkv[:, 2 * width :].T, heads, first_distance, table_heads
    )
    mixed_one = base_all + dot_tt(gather_rows(kept_one), self_out_full_t)
    norm_two, inverse_two = rms_forward(mixed_one, gain_cross)
    key_value = matmul(enc_all, cross_key_value).astype(jnp.bfloat16)
    query_two = jnp.concatenate(
        [matmul(norm_two, cross_query_local).astype(jnp.bfloat16), query_mark], axis=1
    )
    key_two = jnp.concatenate([key_value[:, :width], key_mark], axis=1)
    value_two = jnp.concatenate([key_value[:, width:], blank], axis=1)
    kept_two, sums_two = attend_forward(query_two, key_two, key_value[:, width:].T, heads)
    mixed_two = mixed_one + dot_tt(gather_rows(kept_two), cross_out_full_t)
    norm_three, inverse_three = rms_forward(mixed_two, gain_ff)
    gate_and_upper = matmul(norm_three, gate_upper)
    gate_value, upper_value = gate_and_upper[:, :units], gate_and_upper[:, units:]
    gelu_value, gelu_pull = jax.vjp(gelu_tanh, gate_value)
    hidden_value = (gelu_value * upper_value).astype(jnp.bfloat16)

    grad_hidden = matmul(cotangent_all, down_t)
    grad_gate = gelu_pull(grad_hidden * upper_value)[0].astype(jnp.bfloat16)
    grad_upper = (grad_hidden * gelu_value).astype(jnp.bfloat16)
    grad_both = jnp.concatenate([grad_gate, grad_upper], axis=1)
    norm_grad_three_terms = dot_nt(grad_both, gate_upper)
    gain_grad_ff = jnp.sum(norm_grad_three_terms * mixed_two * inverse_three, axis=0)
    norm_grad_three = scatter_rows(norm_grad_three_terms)
    cotangent_two = d_out.astype(jnp.float32) + rms_backward(
        own_rows(mixed_two), own_rows(inverse_three), gain_ff, norm_grad_three
    )
    cotangent_two_all = gather_rows(cotangent_two.astype(jnp.bfloat16))
    output = (own_rows(mixed_two) + scatter_rows(dot_nt(hidden_value, down_t))).astype(jnp.bfloat16)
    ff_grads = scatter_grads((dot_tn(norm_three, grad_both), dot_tn(cotangent_all, hidden_value)))

    grad_att_two = matmul(cotangent_two_all, cross_out_t).astype(jnp.bfloat16)
    grad_query_two, grad_key_two, grad_value_two = attend_backward(
        query_two,
        key_two,
        key_two[:, :width].T,
        value_two,
        jnp.concatenate([grad_att_two, blank], axis=1),
        sums_two,
        heads,
    )
    grad_kv_two = jnp.concatenate([grad_key_two[:, :width], grad_value_two[:, :width]], axis=1)
    norm_grad_two = dot_tt(gather_rows(grad_query_two), cross_query_full)
    grad_enc = scatter_rows(dot_nt(grad_kv_two, cross_key_value)).astype(jnp.bfloat16)
    back_two = rms_backward(mixed_one, inverse_two, gain_cross, norm_grad_two)
    gain_grad_cross = jnp.sum(
        own_rows(norm_grad_two) * own_rows(mixed_one) * own_rows(inverse_two), axis=0
    )
    cotangent_one = cotangent_two + own_rows(back_two)
    cotangent_one_all = (cotangent_two_all.astype(jnp.float32) + back_two).astype(jnp.bfloat16)
    cross_grads = scatter_grads(
        (
            dot_rows(norm_two, grad_query_two),
            dot_tn(enc_all, grad_kv_two),
            dot_rows(cotangent_two_all, kept_two),
        )
    )

    grad_att_one = matmul(cotangent_one_all, self_out_t).astype(jnp.bfloat16)
    grad_query_one, grad_key_one, grad_value_one, reached = attend_backward(
        query_one,
        key_one,
        key_one[:, :width].T,
        value_one,
        jnp.concatenate([grad_att_one, blank], axis=1),
        sums_one,
        heads,
        first_distance,
        band,
    )
    grad_kv_one = jnp.concatenate([grad_key_one[:, :width], grad_value_one[:, :width]], axis=1)
    norm_grad_one_terms = dot_tt(grad_query_one, first_weights[:, :width]) + dot_nt(
        grad_kv_one, first_weights[:, width:]
    )
    gain_grad_self = jnp.sum(norm_grad_one_terms * base_all * inverse_one, axis=0)
    norm_grad_one = scatter_rows(norm_grad_one_terms)
    grad_hidden_in = (
        cotangent_one
        + rms_backward(own_rows(base_all), own_rows(inverse_one), gain_self, norm_grad_one)
    ).astype(jnp.bfloat16)
    self_grads = scatter_grads(
        (
            dot_rows(norm_one, grad_query_one),
            dot_tn(norm_one, grad_kv_one),
            dot_rows(cotangent_one_all, kept_one),
        )
    )
    at_least = jnp.sum(reached, axis=2)
    grad_table = at_least - jnp.pad(at_least[:, 1:], ((0, 0), (0, 1)))
    table_full = lax.dynamic_update_slice_in_dim(
        jnp.zeros(rel_table.shape, jnp.float32), grad_table.T, place * heads, 1
    )
    small = jnp.concatenate(
        [gain_grad_self, gain_grad_cross, gain_grad_ff, table_full.reshape(-1)]
    )
    small = lax.psum(small, ("dp", "tensor"))
    return (
        output,
        grad_hidden_in,
        grad_enc,
        small[:model],
        small[model : 2 * model],
        small[2 * model : 3 * model],
        small[3 * model :].reshape(rel_table.shape),
        self_grads[:, :width],
        self_grads[:, width : 2 * width],
        self_grads[:, 2 * width : 3 * width],
        self_grads[:, 3 * width :].T,
        cross_grads[:, :width],
        cross_grads[:, width : 2 * width],
        cross_grads[:, 2 * width : 3 * width],
        cross_grads[:, 3 * width :].T,
        ff_grads[:, :units],
        ff_grads[:, units : 2 * units],
        ff_grads[:, 2 * units :].T,
    )


def solution(mesh):
    return jax.shard_map(
        local,
        mesh=mesh,
        in_specs=(
            P(("dp", "tensor"), None),
            P(("dp", "tensor"), None),
            P("dp"),
            P(),
            P(),
            P(),
            P(),
            P(),
            P("dp", "tensor"),
            P("dp", "tensor"),
            P("dp", "tensor"),
            P("tensor", "dp"),
            P("dp", "tensor"),
            P("dp", "tensor"),
            P("dp", "tensor"),
            P("tensor", "dp"),
            P("dp", "tensor"),
            P("dp", "tensor"),
            P("tensor", "dp"),
            P(("dp", "tensor"), None),
        ),
        out_specs=(
            P(("dp", "tensor"), None),
            P(("dp", "tensor"), None),
            P(("dp", "tensor"), None),
            P(),
            P(),
            P(),
            P(),
            P("dp", "tensor"),
            P("dp", "tensor"),
            P("dp", "tensor"),
            P("tensor", "dp"),
            P("dp", "tensor"),
            P("dp", "tensor"),
            P("dp", "tensor"),
            P("tensor", "dp"),
            P("dp", "tensor"),
            P("dp", "tensor"),
            P("tensor", "dp"),
        ),
        check_vma=False,
    )
```
